32 devices in a mesh: section: 2 (over core), dp: 4 (over z), tensor: 4 (over y, x).
Axes of the slice: x: 2, y: 2, z: 4, core: 2. Of those that a mesh axis runs over, the one named last changes fastest.
Arguments:
- block_input: bfloat16 [8, 256, 768], P('dp', 'tensor'), may hold values from -6 to 6
- condition: bfloat16 [8, 768], P('dp'), may hold values from -6 to 6
- out_grad: bfloat16 [8, 256, 768], P('dp', 'tensor'), may hold values from -6 to 6
- live_count: int32 [4], P('dp'), may hold values from 1 to 2, as said below
- ada_weight: bfloat16 [2, 768, 6, 768], P('section', 'dp', None, 'tensor'), may hold values from -0.21875 to 0.21875
- ada_bias: bfloat16 [2, 6, 768], P('section', None, 'tensor'), may hold values from -3 to 3
- qkv_weight: bfloat16 [2, 3, 768, 768], P('section', None, 'dp', 'tensor'), may hold values from -0.21875 to 0.21875
- qv_bias: bfloat16 [2, 2, 768], P('section', None, 'tensor'), may hold values from -2 to 2
- out_weight: bfloat16 [2, 768, 768], P('section', 'tensor', 'dp'), may hold values from -0.875 to 0.875
- out_bias: bfloat16 [2, 768], P('section', 'tensor'), may hold values from -2 to 2
- up_weight: bfloat16 [2, 768, 3072], P('section', 'dp', 'tensor'), may hold values from -0.21875 to 0.21875
- up_bias: bfloat16 [2, 3072], P('section', 'tensor'), may hold values from -2 to 2
- down_weight: bfloat16 [2, 3072, 768], P('section', 'tensor', 'dp'), may hold values from -0.109375 to 0.109375
- down_bias: bfloat16 [2, 768], P('section', 'tensor'), may hold values from -2 to 2
Outputs:
- activations: bfloat16 [2, 8, 256, 768], P('section', 'dp', 'tensor')
- input_grads: bfloat16 [2, 8, 256, 768], P('section', 'dp', 'tensor')
- ada_weight_grad: float32 [2, 768, 6, 768], P('section', 'dp', None, 'tensor')
- ada_bias_grad: float32 [2, 6, 768], P('section', None, 'tensor')
- qkv_weight_grad: float32 [2, 3, 768, 768], P('section', None, 'dp', 'tensor')
- qv_bias_grad: float32 [2, 2, 768], P('section', None, 'tensor')
- out_weight_grad: float32 [2, 768, 768], P('section', 'tensor', 'dp')
- out_bias_grad: float32 [2, 768], P('section', 'tensor')
- up_weight_grad: float32 [2, 768, 3072], P('section', 'dp', 'tensor')
- up_bias_grad: float32 [2, 3072], P('section', 'tensor')
- down_weight_grad: float32 [2, 3072, 768], P('section', 'tensor', 'dp')
- down_bias_grad: float32 [2, 768], P('section', 'tensor')
The draws below stay inside these ranges and needn't reach their ends.
Inputs may be any that keep to these rules, and one draw needn't show every extreme that they name: `live_count`: slots below a device's count are live; some device has all 2 slots live.
All inputs are finite; a program needn't handle non-finite values.
Results may differ from the reference program's by a relative error of at most 0.024.
Values may be sent and summed in bfloat16 or wider, within the bound.
A program may use at most 128 MiB of HBM per device.

```python
import math
import jax
import jax.numpy as jnp
from jax import lax

D = 768
HEADS = 12
HEAD_DIM = 64
FF = 3072
SEQ = 256
SECTIONS = 2
LAT_DEV = 2
LATENTS = 8
N_DP = 4


def draw_live_count(key, part):
    key = jax.random.fold_in(key, 11)
    first_key, second_key = jax.random.split(key)
    counts = jax.random.randint(first_key, (N_DP,), 1, LAT_DEV + 1)
    full_device = jax.random.randint(second_key, (), 0, N_DP)
    return jnp.where(jnp.arange(N_DP) == full_device, LAT_DEV, counts).astype(jnp.int32)


def block_levels(stream_key, shape, shards, low, top_value):
    def one(position, parts):
        draws = jax.random.uniform(jax.random.fold_in(jax.random.fold_in(stream_key, 6), position), (parts,), jnp.float32, low / len(shards), top_value / len(shards))
        return jnp.repeat(jnp.exp(draws), shape[position] // parts).reshape((-1,) + (1,) * (len(shape) - position - 1))

    level = one(*shards[0])
    for cut in shards[1:]:
        level = level * one(*cut)
    return level


def normal_values(own_key, dims, scale, limit, shards=(), kind=jnp.bfloat16):
    drawn = jax.random.normal(own_key, dims, jnp.float32) * scale
    if len(shards) > 0:
        drawn = block_levels(own_key, dims, shards, -0.22, 0.18) * drawn
    return jnp.clip(drawn, min=-limit, max=limit).astype(kind)


def setup_inputs(seed: int = 0) -> dict:
    seeds = jax.random.split(jax.random.key(seed), 15)
    return {
        "block_input": normal_values(seeds[0], (LATENTS, SEQ, D), 1.0, 6.0, ((0, 4), (1, 4))),
        "condition": normal_values(seeds[1], (LATENTS, D), 1.0, 6.0, ((0, 4),)),
        "out_grad": normal_values(seeds[2], (LATENTS, SEQ, D), 1.0, 6.0, ((0, 4), (1, 4))),
        "live_count": draw_live_count(jax.random.fold_in(seeds[14], 71), 0),
        "ada_weight": normal_values(seeds[4], (SECTIONS, D, 6, D), D ** -0.5, 0.21875, ((0, 2), (1, 4), (3, 4))),
        "ada_bias": normal_values(seeds[5], (SECTIONS, 6, D), 0.5, 3.0, ((0, 2), (2, 4))),
        "qkv_weight": normal_values(seeds[6], (SECTIONS, 3, D, D), D ** -0.5, 0.21875, ((0, 2), (2, 4), (3, 4))),
        "qv_bias": normal_values(seeds[7], (SECTIONS, 2, D), 0.3, 2.0, ((0, 2), (2, 4))),
        "out_weight": normal_values(seeds[8], (SECTIONS, D, D), (D // 16) ** -0.5, 0.875, ((0, 2), (1, 4), (2, 4))),
        "out_bias": normal_values(seeds[9], (SECTIONS, D), 0.3, 2.0, ((0, 2), (1, 4))),
        "up_weight": normal_values(seeds[10], (SECTIONS, D, FF), D ** -0.5, 0.21875, ((0, 2), (1, 4), (2, 4))),
        "up_bias": normal_values(seeds[11], (SECTIONS, FF), 0.3, 2.0, ((0, 2), (1, 4))),
        "down_weight": normal_values(seeds[12], (SECTIONS, FF, D), FF ** -0.5, 0.109375, ((0, 2), (1, 4), (2, 4))),
        "down_bias": normal_values(seeds[13], (SECTIONS, D), 0.3, 2.0, ((0, 2), (1, 4))),
    }


@jax.custom_vjp
def low(v):
    return lax.optimization_barrier(v.astype(jnp.bfloat16)).astype(jnp.float32)

@jax.custom_vjp
def lowered_backward(v):
    return v

def low_keep(v):
    return (low(v), None)

def low_pass(kept, grad):
    return (grad,)

def back_keep(v):
    return (v, None)

def back_low(kept, grad):
    return (low(grad),)
low.defvjp(low_keep, low_pass)
lowered_backward.defvjp(back_keep, back_low)
highest_precision = lax.Precision.HIGHEST
epsilon = 1e-06

def norm_rows(values):
    center = values - lax.optimization_barrier(jnp.mean(values, axis=-1, keepdims=True))
    return center * lax.rsqrt(lax.optimization_barrier(jnp.mean(center * center, axis=-1, keepdims=True)) + epsilon)

def gelu_tanh(values):
    return jax.nn.gelu(values, approximate=True)

def layer(residual_in, cond, params):
    ada_w, ada_b, qkv_w, qv_b, out_w, out_b, up_projection_weight, up_projection_bias, down_projection_weight, down_projection_bias = params
    latents = residual_in.shape[0]
    scaling = 1.0 / math.sqrt(HEAD_DIM)
    activated = low(jax.nn.silu(cond))
    modulation = jnp.einsum('ld,dke->lke', activated, ada_w, precision=highest_precision) + ada_b
    pieces = [modulation[:, column][:, None, :] for column in range(6)]
    shift_in, scale_in, gate_in, shift_mid, scale_mid, gate_mid = pieces
    modulated = low(norm_rows(residual_in) * (1.0 + scale_in) + shift_in)
    bias_rows = jnp.stack([qv_b[0], jnp.zeros_like(qv_b[0]), qv_b[1]])
    triple = jnp.einsum('lsd,kde->klse', modulated, qkv_w, precision=highest_precision) + bias_rows[:, None, None, :]
    triple = low(lowered_backward(triple)).reshape(3, latents, SEQ, HEADS, HEAD_DIM)
    scores = lowered_backward(jnp.einsum('lqhe,lkhe->lhqk', triple[0], triple[1], precision=highest_precision) * scaling)
    probs = low(jax.nn.softmax(scores, axis=-1))
    mixed = jnp.einsum('lhqk,lkhe->lqhe', probs, triple[2], precision=highest_precision)
    mixed = low(lowered_backward(mixed)).reshape(latents, SEQ, D)
    attended = lowered_backward(jnp.einsum('lsd,de->lse', mixed, out_w, precision=highest_precision) + out_b)
    middle = residual_in + gate_in * attended
    modulated_middle = low(norm_rows(low(middle)) * (1.0 + scale_mid) + shift_mid)
    hidden_before_gelu = lowered_backward(jnp.einsum('nzp,pe->nze', modulated_middle, up_projection_weight, precision=highest_precision) + up_projection_bias)
    hidden_state = low(gelu_tanh(hidden_before_gelu))
    branch_output = lowered_backward(jnp.einsum('qtv,vh->qth', hidden_state, down_projection_weight, precision=highest_precision) + down_projection_bias)
    return middle + gate_mid * branch_output

def reference(block_input, condition, out_grad, live_count, ada_weight, ada_bias, qkv_weight, qv_bias, out_weight, out_bias, up_weight, up_bias, down_weight, down_bias):
    params = (ada_weight, ada_bias, qkv_weight, qv_bias, out_weight, out_bias, up_weight, up_bias, down_weight, down_bias)
    first_params = tuple((item[0].astype(jnp.float32) for item in params))
    second_params = tuple((item[1].astype(jnp.float32) for item in params))
    slot_index = jnp.arange(LATENTS, dtype=jnp.int32) % LAT_DEV
    live_mask = (slot_index < jnp.repeat(live_count, LAT_DEV)).astype(jnp.float32)
    group_size = LAT_DEV * min(N_DP, 8)
    group_count = LATENTS // group_size
    grouped = (block_input.reshape(group_count, group_size, SEQ, D), condition.reshape(group_count, group_size, D), out_grad.reshape(group_count, group_size, SEQ, D), live_mask.reshape(group_count, group_size))
    initial = tuple((jnp.zeros(item.shape, jnp.float32) for item in params))

    def group_step(totals, item):
        inputs_now, cond_now, grad_now, mask_now = item
        cond_float = cond_now.astype(jnp.float32)

        def apply_layer(values, weights):
            return layer(values, cond_float, weights)
        first_out, first_back = jax.vjp(apply_layer, inputs_now.astype(jnp.float32), first_params)
        first_low = first_out.astype(jnp.bfloat16)
        second_out, second_back = jax.vjp(apply_layer, first_low.astype(jnp.float32), second_params)
        cotangent = grad_now.astype(jnp.float32) * mask_now[:, None, None]
        middle_grad, second_grads = second_back(cotangent)
        middle_low = middle_grad.astype(jnp.bfloat16)
        input_grad, first_grads = first_back(middle_low.astype(jnp.float32))

        def add_both(total, grad_first, grad_second):
            return total + jnp.stack([grad_first, grad_second])
        totals = jax.tree.map(add_both, totals, first_grads, second_grads)
        return (totals, (first_low, second_out.astype(jnp.bfloat16), input_grad.astype(jnp.bfloat16), middle_low))
    totals, results = lax.scan(group_step, initial, grouped)
    first_act = results[0].reshape(LATENTS, SEQ, D)
    second_act = results[1].reshape(LATENTS, SEQ, D)
    first_grad = results[2].reshape(LATENTS, SEQ, D)
    second_grad = results[3].reshape(LATENTS, SEQ, D)
    activations = jnp.stack([first_act, second_act])
    input_grads = jnp.stack([first_grad, second_grad])
    return (activations, input_grads, totals[0], totals[1], totals[2], totals[3], totals[4], totals[5], totals[6], totals[7], totals[8], totals[9])
```

```python
import functools
import math

import jax
import jax.numpy as jnp
from jax import lax
from jax.experimental import pallas as pl
from jax.experimental.pallas import tpu as pltpu
from jax.sharding import PartitionSpec as P

HEAD_DIM = 64
epsilon = 1e-06
MESH = pl.DeviceIdType.MESH
F32 = jnp.float32
BF16 = jnp.bfloat16
GELU_C = math.sqrt(2.0 / math.pi)
VMEM_LIMIT = 56 * 1024 * 1024


def dot(a, b):
    return jnp.dot(a, b, preferred_element_type=F32)


def dot_t(a, b):
    return lax.dot_general(a, b, (((1,), (1,)), ((), ())), preferred_element_type=F32)


def t_dot(a, b):
    return lax.dot_general(a, b, (((0,), (0,)), ((), ())), preferred_element_type=F32)


def norm_rows(values):
    center = values - jnp.mean(values, axis=-1, keepdims=True)
    spread = lax.rsqrt(jnp.mean(center * center, axis=-1, keepdims=True) + epsilon)
    return center * spread, spread


def norm_back(grad_hat, own_hat, spread):
    first_mean = jnp.mean(grad_hat, axis=-1, keepdims=True)
    second_mean = jnp.mean(grad_hat * own_hat, axis=-1, keepdims=True)
    return spread * (grad_hat - first_mean - own_hat * second_mean)


def ring_peer(axis, me, k, n):
    return lax.rem(me + k, n)


def greet(axes_peers):
    barrier = pltpu.get_barrier_semaphore()
    for peer in axes_peers:
        pl.semaphore_signal(barrier, inc=1, device_id=peer, device_id_type=MESH)
    pl.semaphore_wait(barrier, len(axes_peers))


class Exchange:
    def __init__(self, n, send, recv):
        self.n, self.send, self.recv = n, send, recv
        self.me = lax.axis_index("tensor")
        self.count = 0

    def _copies(self, src_of, dst_of):
        base = self.count * (self.n - 1)
        self.count += 1
        copies = []
        for k in range(1, self.n):
            peer = lax.rem(self.me + k, self.n)
            copy = pltpu.make_async_remote_copy(
                src_ref=src_of(peer),
                dst_ref=dst_of(k),
                send_sem=self.send.at[base + k - 1],
                recv_sem=self.recv.at[base + k - 1],
                device_id={"tensor": peer},
                device_id_type=MESH,
            )
            copy.start()
            copies.append(copy)
        return copies

    def gather(self, buf, own):
        buf[self.me] = own
        return self._copies(lambda peer: buf.at[self.me], lambda k: buf.at[self.me])

    def scatter(self, sbuf, rbuf):
        return self._copies(lambda peer: sbuf.at[peer], lambda k: rbuf.at[k - 1])


def finish(copies):
    for copy in copies:
        copy.wait()


def flat(ref):
    value = ref[...]
    return value.reshape(value.shape[0] * value.shape[1], value.shape[2])


def put_parts(total, keep, sbuf):
    shaped = total.reshape(sbuf.shape)
    keep[...] = shaped
    sbuf[...] = shaped.astype(BF16)


def head_masks(width):
    lane = lax.broadcasted_iota(jnp.int32, (1, width), 1)
    return [
        jnp.logical_and(lane >= h * HEAD_DIM, lane < (h + 1) * HEAD_DIM)
        for h in range(width // HEAD_DIM)
    ]


def pick(mask, value):
    return jnp.where(mask, value, jnp.zeros_like(value))


def forward_kernel(
    n,
    x_ref, mod_ref, wqkv, wout, wup, wdown, bqkv, bup, brow,
    y_ref, m1_ref, qkv_ref, o_ref, att_ref, x1_ref, m2_ref, hpre_ref, f_ref,
    keep, sbuf, rbuf, send, recv,
):
    ex = Exchange(n, send, recv)
    greet([{"tensor": lax.rem(ex.me + k, n)} for k in range(1, n)])
    x = x_ref[...].astype(F32)
    mod = mod_ref[...]
    scaling = 1.0 / math.sqrt(HEAD_DIM)
    hat, _ = norm_rows(x)
    finish(ex.gather(m1_ref, (hat * (1.0 + mod[1:2]) + mod[0:1]).astype(BF16)))
    m1 = flat(m1_ref)
    triple = []
    for j in range(3):
        part = (dot(m1, wqkv[j]) + bqkv[j : j + 1, :]).astype(BF16)
        qkv_ref[j] = part
        triple.append(part)
    q, k, v = triple
    mixed = None
    for mask in head_masks(q.shape[1]):
        s = dot_t(pick(mask, q), k) * scaling
        e = jnp.exp(s - jnp.max(s, axis=-1, keepdims=True))
        p = (e / jnp.sum(e, axis=-1, keepdims=True)).astype(BF16)
        o = dot(p, pick(mask, v))
        mixed = o if mixed is None else mixed + o
    mixed = mixed.astype(BF16)
    o_ref[...] = mixed
    put_parts(dot(mixed, wout[...]), keep, sbuf.at[0])
    finish(ex.scatter(sbuf.at[0], rbuf.at[0]))
    att = keep[ex.me] + brow[0:1, :]
    for i in range(n - 1):
        att = att + rbuf[0, i].astype(F32)
    att_ref[...] = att
    x1 = x + mod[2:3] * att
    x1_ref[...] = x1
    hat2, _ = norm_rows(x1.astype(BF16).astype(F32))
    finish(ex.gather(m2_ref, (hat2 * (1.0 + mod[4:5]) + mod[3:4]).astype(BF16)))
    hpre = dot(flat(m2_ref), wup[...]) + bup[...]
    hpre_ref[...] = hpre
    t = jnp.tanh(GELU_C * (hpre + 0.044715 * (hpre * hpre * hpre)))
    hidden = (0.5 * hpre * (1.0 + t)).astype(BF16)
    put_parts(dot(hidden, wdown[...]), keep, sbuf.at[1])
    finish(ex.scatter(sbuf.at[1], rbuf.at[1]))
    f = keep[ex.me] + brow[1:2, :]
    for i in range(n - 1):
        f = f + rbuf[1, i].astype(F32)
    f_ref[...] = f
    y_ref[...] = (x1 + mod[5:6] * f).astype(BF16)


def backward_kernel(
    n, nd,
    dy_ref, x_ref, mod_ref, wqkv, wout, wup, wdown,
    m1_ref, qkv_ref, o_ref, att_ref, x1_ref, m2_ref, hpre_ref, f_ref,
    dx_ref, dqkv_ref, dout_ref, dup_ref, ddown_ref, small_ref, bias_ref,
    gbuf, keep, sbuf, rbuf, tbuf, trecv, send, recv,
):
    ex = Exchange(n, send, recv)
    greet([{"tensor": lax.rem(ex.me + k, n)} for k in range(1, n)])
    mod = mod_ref[...]
    scaling = 1.0 / math.sqrt(HEAD_DIM)

    def row_sum(value):
        return jnp.sum(value, axis=0, keepdims=True)

    res = dy_ref[...].astype(F32)
    dgate2 = row_sum(res * f_ref[...])
    branch = (mod[5:6] * res).astype(BF16)
    ddown_b = row_sum(branch.astype(F32))
    copies = ex.gather(gbuf.at[0], branch)
    hpre = hpre_ref[...]
    square = hpre * hpre
    t = jnp.tanh(GELU_C * (hpre + 0.044715 * (square * hpre)))
    hidden = (0.5 * hpre * (1.0 + t)).astype(BF16)
    slope = 0.5 * (1.0 + t) + (0.5 * GELU_C) * hpre * (1.0 - t * t) * (
        1.0 + 3.0 * 0.044715 * square
    )
    finish(copies)
    branch_full = flat(gbuf.at[0])
    dpre_f = dot_t(branch_full, wdown[...]) * slope
    dpre = dpre_f.astype(BF16)
    put_parts(dot_t(dpre, wup[...]), keep, sbuf.at[0])
    copies = ex.scatter(sbuf.at[0], rbuf.at[0])
    bias_ref[0:1, :] = row_sum(dpre.astype(F32))
    width = ddown_ref.shape[2]
    rows = dup_ref.shape[1]
    grad_down = t_dot(hidden, branch_full).astype(BF16)
    for d in range(nd):
        ddown_ref[d] = grad_down[:, d * width : (d + 1) * width]
    grad_up = t_dot(flat(m2_ref), dpre)
    for d in range(nd):
        dup_ref[d] = grad_up[d * rows : (d + 1) * rows, :].astype(BF16)
    finish(copies)
    dm2 = keep[ex.me]
    for i in range(n - 1):
        dm2 = dm2 + rbuf[0, i].astype(F32)
    hat2, spread2 = norm_rows(x1_ref[...].astype(BF16).astype(F32))
    dscale2 = row_sum(dm2 * hat2)
    dshift2 = row_sum(dm2)
    res = res + norm_back(dm2 * (1.0 + mod[4:5]), hat2, spread2)
    dgate1 = row_sum(res * att_ref[...])
    attn = (mod[2:3] * res).astype(BF16)
    dout_b = row_sum(attn.astype(F32))
    copies = ex.gather(gbuf.at[1], attn)
    q, k, v = qkv_ref[0], qkv_ref[1], qkv_ref[2]
    masks = head_masks(q.shape[1])
    probs = []
    for mask in masks:
        s = dot_t(pick(mask, q), k) * scaling
        e = jnp.exp(s - jnp.max(s, axis=-1, keepdims=True))
        probs.append(e / jnp.sum(e, axis=-1, keepdims=True))
    finish(copies)
    attn_full = flat(gbuf.at[1])
    dmix = dot_t(attn_full, wout[...]).astype(BF16)
    dq = dk = dv = None
    for mask, p in zip(masks, probs):
        own = pick(mask, dmix)
        dp = dot_t(own, v)
        ds = (p * (dp - jnp.sum(dp * p, axis=-1, keepdims=True))).astype(BF16)
        dvh = t_dot(p.astype(BF16), own)
        dqh = dot(ds, pick(mask, k))
        dkh = t_dot(ds, pick(mask, q))
        dq = dqh if dq is None else dq + dqh
        dk = dkh if dk is None else dk + dkh
        dv = dvh if dv is None else dv + dvh
    dz = [(dq * scaling).astype(BF16), (dk * scaling).astype(BF16), dv.astype(BF16)]
    dm1 = dot_t(dz[0], wqkv[0]) + dot_t(dz[1], wqkv[1]) + dot_t(dz[2], wqkv[2])
    put_parts(dm1, keep, sbuf.at[1])
    copies = ex.scatter(sbuf.at[1], rbuf.at[1])
    local = q.shape[1]
    bias_ref[1:2, 0:local] = row_sum(dz[0].astype(F32))
    bias_ref[2:3, 0:local] = row_sum(dz[2].astype(F32))
    grad_out = t_dot(o_ref[...], attn_full).astype(BF16)
    width = dout_ref.shape[2]
    for d in range(nd):
        dout_ref[d] = grad_out[:, d * width : (d + 1) * width]
    m1 = flat(m1_ref)
    rows = dqkv_ref.shape[2]
    for j in range(3):
        grad_j = t_dot(m1, dz[j])
        for d in range(nd):
            dqkv_ref[d, j] = grad_j[d * rows : (d + 1) * rows, :].astype(BF16)
    finish(copies)
    dm1_own = keep[ex.me]
    for i in range(n - 1):
        dm1_own = dm1_own + rbuf[1, i].astype(F32)
    hat, spread = norm_rows(x_ref[...].astype(F32))
    dscale1 = row_sum(dm1_own * hat)
    dshift1 = row_sum(dm1_own)
    dx_ref[...] = (res + norm_back(dm1_own * (1.0 + mod[1:2]), hat, spread)).astype(BF16)
    small = [dshift1, dscale1, dgate1, dshift2, dscale2, dgate2, dout_b, ddown_b]
    cut = tbuf.shape[2]
    for t_index in range(n):
        for r, row in enumerate(small):
            tbuf[t_index, r : r + 1, :] = row[:, t_index * cut : (t_index + 1) * cut]
    finish(ex.scatter(tbuf, trecv))
    total = tbuf[ex.me]
    for i in range(n - 1):
        total = total + trecv[i]
    small_ref[...] = total


def vmem(count):
    return [pl.BlockSpec(memory_space=pltpu.VMEM)] * count


def sds(shape, dtype):
    return jax.ShapeDtypeStruct(shape, dtype)


def call_forward(n, x, mod, weights, bqkv, bup, brow):
    tokens, width = x.shape
    local = weights[0].shape[2]
    hidden = weights[2].shape[1]
    rows = n * tokens
    parts = (n, tokens, width)
    return pl.pallas_call(
        functools.partial(forward_kernel, n),
        out_shape=(
            sds((tokens, width), BF16),
            sds(parts, BF16),
            sds((3, rows, local), BF16),
            sds((rows, local), BF16),
            sds((tokens, width), F32),
            sds((tokens, width), F32),
            sds(parts, BF16),
            sds((rows, hidden), F32),
            sds((tokens, width), F32),
        ),
        in_specs=vmem(9),
        out_specs=tuple(vmem(9)),
        scratch_shapes=[
            pltpu.VMEM(parts, F32),
            pltpu.VMEM((2,) + parts, BF16),
            pltpu.VMEM((2, n - 1, tokens, width), BF16),
            pltpu.SemaphoreType.DMA((4 * (n - 1),)),
            pltpu.SemaphoreType.DMA((4 * (n - 1),)),
        ],
        compiler_params=pltpu.CompilerParams(
            collective_id=0, has_side_effects=True, vmem_limit_bytes=VMEM_LIMIT
        ),
        cost_estimate=pl.CostEstimate(
            flops=20_000_000_000, bytes_accessed=6_000_000, transcendentals=0
        ),
        name="layer_forward",
    )(x, mod, *weights, bqkv, bup, brow)


def call_backward(n, nd, dy, x, mod, weights, stored):
    tokens, width = x.shape
    local = weights[0].shape[2]
    hidden = weights[2].shape[1]
    parts = (n, tokens, width)
    cut = width // n
    own = width // nd
    return pl.pallas_call(
        functools.partial(backward_kernel, n, nd),
        out_shape=(
            sds((tokens, width), BF16),
            sds((nd, 3, own, local), BF16),
            sds((nd, local, own), BF16),
            sds((nd, own, hidden), BF16),
            sds((nd, hidden, own), BF16),
            sds((8, cut), F32),
            sds((3, hidden), F32),
        ),
        in_specs=vmem(15),
        out_specs=tuple(vmem(7)),
        scratch_shapes=[
            pltpu.VMEM((2,) + parts, BF16),
            pltpu.VMEM(parts, F32),
            pltpu.VMEM((2,) + parts, BF16),
            pltpu.VMEM((2, n - 1, tokens, width), BF16),
            pltpu.VMEM((n, 8, cut), F32),
            pltpu.VMEM((n - 1, 8, cut), F32),
            pltpu.SemaphoreType.DMA((5 * (n - 1),)),
            pltpu.SemaphoreType.DMA((5 * (n - 1),)),
        ],
        compiler_params=pltpu.CompilerParams(
            collective_id=1, has_side_effects=True, vmem_limit_bytes=VMEM_LIMIT
        ),
        cost_estimate=pl.CostEstimate(
            flops=30_000_000_000, bytes_accessed=10_000_000, transcendentals=0
        ),
        name="layer_backward",
    )(dy, x, mod, *weights, *stored)


def on_device(
    block_input, condition, out_grad, live_count, ada_weight, ada_bias, qkv_weight, qv_bias,
    out_weight, out_bias, up_weight, up_bias, down_weight, down_bias,
):
    section = lax.axis_index("section")
    ns = lax.axis_size("section")
    nd = lax.axis_size("dp")
    n = lax.axis_size("tensor")
    dp_index = lax.axis_index("dp")
    slots, tokens, width = block_input.shape

    own_layer = (
        lax.all_gather(qkv_weight[0], "dp", axis=1, tiled=True),
        lax.all_gather(out_weight[0], "dp", axis=1, tiled=True),
        lax.all_gather(up_weight[0], "dp", axis=0, tiled=True),
        lax.all_gather(down_weight[0], "dp", axis=1, tiled=True),
    )
    both = tuple(lax.all_gather(item, "section", axis=0) for item in own_layer)
    weights = [tuple(item[s] for item in both) for s in range(ns)]

    act = jax.nn.silu(condition.astype(F32)).astype(BF16)
    act_all = lax.all_gather(act, "dp", axis=0, tiled=True)
    own_rows = ada_weight.shape[1]
    act_rows = lax.dynamic_slice_in_dim(act_all, dp_index * own_rows, own_rows, 1)
    mod_part = jnp.einsum("ld,dke->lke", act_rows, ada_weight[0], preferred_element_type=F32)
    mod_cut = lax.psum_scatter(mod_part, "dp", scatter_dimension=0, tiled=True)
    mod_cut = mod_cut + ada_bias[0].astype(F32)
    cut = mod_cut.shape[2]
    local = qv_bias.shape[2]
    pack = jnp.concatenate(
        [
            mod_cut.reshape(slots * 6, cut),
            out_bias.astype(F32),
            down_bias.astype(F32),
            qv_bias[0].astype(F32),
            up_bias[0].astype(F32).reshape(-1, cut),
        ],
        axis=0,
    )
    packs = lax.all_gather(pack, ("section", "tensor"), axis=0).reshape(ns, n, *pack.shape)
    lead = slots * 6
    full = packs[:, :, : lead + 2].transpose(0, 2, 1, 3).reshape(ns, lead + 2, width)
    mod_all = full[:, :lead].reshape(ns, slots, 6, width)
    mod_own = lax.dynamic_index_in_dim(mod_all, section, 1, keepdims=False)
    mine = lax.dynamic_index_in_dim(packs, lax.axis_index("tensor"), 1, keepdims=False)
    zero_row = jnp.zeros((1, local), F32)

    x = lax.dynamic_index_in_dim(block_input, section, 0, keepdims=False)
    live = (section < live_count[0]).astype(F32)
    dy = lax.dynamic_index_in_dim(out_grad, section, 0, keepdims=False)
    dy = (dy.astype(F32) * live).astype(BF16)

    xs, ys, stores = [], [], []
    for s in range(ns):
        qv = mine[s, lead + 2 : lead + 4]
        bqkv = jnp.concatenate([qv[0:1], zero_row, qv[1:2]], axis=0)
        bup = mine[s, lead + 4 :].reshape(1, -1)
        brow = full[s, lead : lead + 2]
        out = call_forward(n, x, mod_own[s], weights[s], bqkv, bup, brow)
        xs.append(x)
        ys.append(out[0])
        stores.append(out[1:])
        x = out[0]
    grads = [None] * ns
    dxs = [None] * ns
    for s in reversed(range(ns)):
        out = call_backward(n, nd, dy, xs[s], mod_own[s], weights[s], stores[s])
        dxs[s] = out[0]
        grads[s] = out[1:]
        dy = out[0]

    def to_owner(items):
        return lax.all_to_all(jnp.stack(items), "section", split_axis=0, concat_axis=0)

    activations = to_owner(ys)
    input_grads = to_owner(dxs)

    def reduced(items):
        pair = to_owner(items)
        summed = (pair[0].astype(F32) + pair[1].astype(F32)).astype(BF16)
        return lax.psum_scatter(summed, "dp", scatter_dimension=0).astype(F32)

    qkv_g, out_g, up_g, down_g = (
        reduced([grads[s][i] for s in range(ns)]) for i in range(4)
    )

    smalls = jnp.stack(
        [
            jnp.concatenate(
                [
                    grads[s][4],
                    grads[s][5][1:3, :local].reshape(-1, cut),
                    grads[s][5][0].reshape(-1, cut),
                ],
                axis=0,
            )
            for s in range(ns)
        ]
    )
    every = lax.all_gather(smalls, ("dp", "section"), axis=0)
    every = lax.dynamic_index_in_dim(every, section, 1, keepdims=False)
    dmod = every[:, :6]
    ada_g = jnp.einsum(
        "ld,lke->dke", act_rows.astype(F32), dmod, precision=lax.Precision.HIGHEST
    )
    totals = jnp.sum(every, axis=0)
    qv_g = totals[8 : 8 + 2 * (local // cut)].reshape(2, local)
    up_b = totals[8 + 2 * (local // cut) :].reshape(-1)
    return (
        activations[None],
        input_grads[None],
        ada_g[None],
        totals[None, :6],
        qkv_g[None],
        qv_g[None],
        out_g[None],
        totals[None, 6],
        up_g[None],
        up_b[None],
        down_g[None],
        totals[None, 7],
    )


def solution(mesh):
    return jax.shard_map(
        on_device,
        mesh=mesh,
        in_specs=(
            P("dp", "tensor", None),
            P("dp", None),
            P("dp", "tensor", None),
            P("dp"),
            P("section", "dp", None, "tensor"),
            P("section", None, "tensor"),
            P("section", None, "dp", "tensor"),
            P("section", None, "tensor"),
            P("section", "tensor", "dp"),
            P("section", "tensor"),
            P("section", "dp", "tensor"),
            P("section", "tensor"),
            P("section", "tensor", "dp"),
            P("section", "tensor"),
        ),
        out_specs=(
            P("section", "dp", "tensor", None),
            P("section", "dp", "tensor", None),
            P("section", "dp", None, "tensor"),
            P("section", None, "tensor"),
            P("section", None, "dp", "tensor"),
            P("section", None, "tensor"),
            P("section", "tensor", "dp"),
            P("section", "tensor"),
            P("section", "dp", "tensor"),
            P("section", "tensor"),
            P("section", "tensor", "dp"),
            P("section", "tensor"),
        ),
        check_vma=False,
    )
```
